256 devices in a mesh: blk: 128 (over y, z_lo, x, core), head: 2 (over z_hi).
Axes of the slice: x: 4, y: 4, z: 8 (z_hi: 2, z_lo: 4; z = z_hi * 4 + z_lo), core: 2. Of those that a mesh axis runs over, the one named last changes fastest.
Arguments:
- queries: bfloat16 [65536, 3584], P(('blk', 'head')), may hold values from -5 to 5
- keys: bfloat16 [65536, 512], P(('blk', 'head')), may hold values from -5 to 5
- values: bfloat16 [65536, 512], P(('blk', 'head')), may hold values from -6 to 6
- kept: int32 [512, 8], P('blk'), may hold values from 0 to 511, as said below
- frame_ids: int32 [65536], replicated, may hold values from 0 to 256, as said below
Outputs:
- attended: bfloat16 [65536, 3584], P(('blk', 'head'))
The draws below stay inside these ranges and needn't reach their ends.
Inputs may be any that keep to these rules, and one draw needn't show every extreme that they name: Row t of kept lists key tiles k with t - 12 < k <= t; its first entry is t; entries may repeat. `frame_ids`: never falls along the sequence; frames begin only at even positions; the first token is in frame 0 and the last frame is 256.
All inputs are finite; a program needn't handle non-finite values.
Results may differ from the reference program's by a relative error of at most 0.008.
Values may be sent and summed in bfloat16 or wider, within the bound.
No kernel may reach another device: no remote copies, remote signals or barrier semaphores. Data moves between devices by JAX's collectives and lax.ppermute only.
A program may use at most 192 MiB of HBM per device.

```python
import math
import jax
import jax.numpy as jnp
from jax import lax

QUERY_HEADS = 28
KEY_VALUE_HEADS = 4
HEAD_SIZE = 128
TOK_DEV = 256
TILE = 128
KMAX = 8
HOPS = 3
SEQUENCE_TOKENS = 65536
QTILES = 512
SPAN = 12
N_BLK = 128
N_HEAD = 2


def draw_keys(key, part):
    key = jax.random.fold_in(key, 11)
    return jax.random.truncated_normal(key, -5.0, 5.0, (SEQUENCE_TOKENS, KEY_VALUE_HEADS * HEAD_SIZE), jnp.float32).astype(jnp.bfloat16)


def draw_queries(key, part):
    key = jax.random.fold_in(key, 17)
    return jax.random.truncated_normal(key, -5.0, 5.0, (SEQUENCE_TOKENS, QUERY_HEADS * HEAD_SIZE), jnp.float32).astype(jnp.bfloat16)


def draw_frame_ids(key, part):
    key = jax.random.fold_in(key, 23)
    pair_list = SEQUENCE_TOKENS // 2
    starts = SEQUENCE_TOKENS // 256
    order = jax.random.permutation(key, pair_list - 1)
    places = order[:starts] + 1
    flags = jnp.zeros((pair_list,), jnp.int32).at[places].set(1)
    return jnp.repeat(jnp.cumsum(flags), 2).astype(jnp.int32)


def draw_kept(key, part):
    key = jax.random.fold_in(key, 37)
    tiles = jnp.arange(QTILES, dtype=jnp.int32)
    offsets = jax.random.randint(key, (QTILES, KMAX - 1), 1, SPAN)
    behind = jnp.maximum(tiles[:, None] - offsets, 0)
    return jnp.concatenate([tiles[:, None], behind], axis=1).astype(jnp.int32)


def shard_levels(stream_key, dims, cuts, smallest, high):
    factor_of, own = 1.0, jax.random.fold_in(stream_key, 6)
    for position, shards_of in cuts:
        heights = jnp.exp(jax.random.uniform(jax.random.fold_in(own, position), (shards_of,), jnp.float32, smallest / len(cuts), high / len(cuts)))
        factor_of = factor_of * jnp.repeat(heights, dims[position] // shards_of).reshape([-1 if axis == position else 1 for axis in range(len(dims))])
    return factor_of


def noise(key, shape, width, limit, shards=(), kind=jnp.bfloat16):
    values = jax.random.normal(key, shape, jnp.float32) * width
    if len(shards) > 0:
        values = shard_levels(key, shape, shards, -0.22, 0.18) * values
    return jnp.clip(values, min=-limit, max=limit).astype(kind)


def setup_inputs(seed: int = 0) -> dict:
    seeds = jax.random.split(jax.random.key(seed), 6)
    queries = draw_queries(jax.random.fold_in(seeds[5], 71), 0)
    keys = draw_keys(jax.random.fold_in(seeds[5], 71), 0)
    values = noise(seeds[2], (SEQUENCE_TOKENS, KEY_VALUE_HEADS * HEAD_SIZE), 1.0, 6.0, ((0, 256),))
    kept = draw_kept(jax.random.fold_in(seeds[5], 71), 0)
    frame_ids = draw_frame_ids(jax.random.fold_in(seeds[5], 71), 0)
    return {"queries": queries, "keys": keys, "values": values, "kept": kept, "frame_ids": frame_ids}


def block_mask(kept_rows, frames_padded, padding_amount, q_start, k_start, random_query_seed, random_key_seed):
    qpos = q_start + jnp.arange(random_query_seed, dtype=jnp.int32)
    kpos = k_start + jnp.arange(random_key_seed, dtype=jnp.int32)
    key_tile = jnp.floor_divide(kpos, TILE)
    tile_hit = jnp.any(kept_rows[:, :, None] == key_tile[None, None, :], axis=1)
    tile_hit = jnp.repeat(tile_hit, TILE, axis=0)
    frame_q = lax.dynamic_slice_in_dim(frames_padded, (q_start + padding_amount).astype(jnp.int32), random_query_seed, 0)
    frame_k = lax.dynamic_slice_in_dim(frames_padded, (k_start + padding_amount).astype(jnp.int32), random_key_seed, 0)
    return tile_hit & (frame_k[None, :] <= frame_q[:, None])

def attend_dense(query_block_tile, key_block_tile, value_block_tile, kept_rows, frames_padded, padding_amount, q_start, k_start):
    random_query_seed = query_block_tile.shape[0]
    random_key_seed = key_block_tile.shape[0]
    group_size = QUERY_HEADS // KEY_VALUE_HEADS
    query_four_dims = query_block_tile.reshape(random_query_seed, KEY_VALUE_HEADS, group_size, HEAD_SIZE).astype(jnp.float32)
    key_three_dims = key_block_tile.reshape(random_key_seed, KEY_VALUE_HEADS, HEAD_SIZE).astype(jnp.float32)
    value_three_dims = value_block_tile.reshape(random_key_seed, KEY_VALUE_HEADS, HEAD_SIZE).astype(jnp.float32)
    scale = 1.0 / math.sqrt(HEAD_SIZE)
    scores = jnp.einsum('qkgd,skd->kgqs', query_four_dims, key_three_dims) * scale
    allowed = block_mask(kept_rows, frames_padded, padding_amount, q_start, k_start, random_query_seed, random_key_seed)
    scores = jnp.where(allowed, scores, -1e+30)
    top = lax.optimization_barrier(jnp.max(scores, axis=-1, keepdims=True))
    expo = jnp.where(allowed, jnp.exp(scores - top), 0.0)
    total = lax.optimization_barrier(jnp.sum(expo, axis=-1, keepdims=True))
    weights = expo.astype(jnp.bfloat16)
    summed = jnp.einsum('kgqs,skd->kgqd', weights.astype(jnp.float32), value_three_dims)
    result = summed / total
    return result.transpose(2, 0, 1, 3).reshape(random_query_seed, QUERY_HEADS * HEAD_SIZE).astype(jnp.bfloat16)

def reference(queries, keys, values, kept, frame_ids):
    block = N_HEAD * TOK_DEV
    tiles = block // TILE
    padding_amount = HOPS * block
    padded_key_rows = jnp.concatenate([jnp.zeros((padding_amount, KEY_VALUE_HEADS * HEAD_SIZE), jnp.bfloat16), keys], axis=0)
    padded_value_rows = jnp.concatenate([jnp.zeros((padding_amount, KEY_VALUE_HEADS * HEAD_SIZE), jnp.bfloat16), values], axis=0)
    frames_padded = jnp.concatenate([jnp.zeros((padding_amount,), jnp.int32), frame_ids], axis=0)

    def one_block(index):
        q_start = (index * block).astype(jnp.int32)
        query_block_tile = lax.dynamic_slice_in_dim(queries, q_start, block, 0)
        key_block_tile = lax.dynamic_slice_in_dim(padded_key_rows, q_start, (HOPS + 1) * block, 0)
        value_block_tile = lax.dynamic_slice_in_dim(padded_value_rows, q_start, (HOPS + 1) * block, 0)
        kept_rows = lax.dynamic_slice_in_dim(kept, (index * tiles).astype(jnp.int32), tiles, 0)
        return attend_dense(query_block_tile, key_block_tile, value_block_tile, kept_rows, frames_padded, padding_amount, q_start, q_start - padding_amount)
    out = lax.map(one_block, jnp.arange(N_BLK, dtype=jnp.int32))
    return out.reshape(SEQUENCE_TOKENS, QUERY_HEADS * HEAD_SIZE)
```

```python
import math

import jax
import jax.numpy as jnp
from jax import lax
from jax.experimental import pallas as pl
from jax.experimental.pallas import tpu as pltpu
from jax.sharding import PartitionSpec as P

QUERY_HEADS = 28
KEY_VALUE_HEADS = 4
GROUP = QUERY_HEADS // KEY_VALUE_HEADS
HEAD_SIZE = 128
TILE = 128
TOKENS = 256
KEPT = 8
BLOCKS = 10
TURN = 16
AXES = ("blk", "head")
HEAD_GROUPS = ((0, 2), (2, 2))
SCALE = math.log2(math.e) / math.sqrt(HEAD_SIZE)
NEVER = -1e30


def device(chip, core, half):
    return (chip * 2 + core) * 2 + half


def across_halves(chips):
    return [
        (device(c, k, h), device(c, k, 1 - h)) for c in range(chips) for k in (0, 1) for h in (0, 1)
    ]


def turns(chip):
    return chip % TURN == 0


def next_chip(chips):
    pairs = []
    for c in range(chips):
        after = (c + 1) % chips
        for k in (0, 1):
            for h in (0, 1):
                pairs.append((device(c, k, h), device(after, k, 1 - h if turns(after) else h)))
    return pairs


def other_core(chips):
    return [
        (device(c, k, h), device(c, 1 - k, h)) for c in range(chips) for k in (0, 1) for h in (0, 1)
    ]


def second_next_chip(chips, halves):
    return [
        (device(c, 1, h), device((c + 2) % chips, 0, h)) for c in range(chips) for h in halves
    ]


def attend_kernel(heads, first_head, *refs):
    where, bias, q, tail, cross_tail = refs[:5]
    blocks = refs[5:13]
    out, keys, values, kept_keys, kept_values = refs[-5:]

    def place(head, slot, block):
        rows = pl.ds(pl.multiple_of(slot * TOKENS, TOKENS), TOKENS)
        keys[head, rows, :] = block[:, :HEAD_SIZE]
        values[head, rows, :] = block[:, HEAD_SIZE:]

    for head in range(heads):
        place(head, 1, cross_tail[:, pl.ds(head * 2 * HEAD_SIZE, 2 * HEAD_SIZE)])
        rows = pl.ds(pl.multiple_of(where[2, 8], TILE), TILE)
        last = tail[:, pl.ds(head * 2 * HEAD_SIZE, 2 * HEAD_SIZE)]
        keys[head, rows, :] = last[:, :HEAD_SIZE]
        values[head, rows, :] = last[:, HEAD_SIZE:]
        for number, block in enumerate(blocks):
            place(head, where[2, number], block[:, pl.ds(head * 2 * HEAD_SIZE, 2 * HEAD_SIZE)])
        for tile in range(2):
            for entry in range(KEPT):
                index = where[tile, entry]
                rows = pl.ds(pl.multiple_of(index * TILE, TILE), TILE)
                slot = pl.ds(entry * TILE, TILE)
                key = keys[head, rows, :]
                value = values[head, rows, :]
                count = jnp.float32(1.0)
                if entry:
                    again = index == where[tile, 0]
                    key = jnp.where(again, jnp.broadcast_to(key[0:1, :], key.shape), key)
                    for earlier in range(1, entry):
                        again = again | (index == where[tile, earlier])
                    value = jnp.where(again, jnp.zeros_like(value), value)
                    count = jnp.where(again, 0.0, 1.0)
                kept_keys[head, tile, slot, :] = key
                kept_values[head, tile, slot, :HEAD_SIZE] = value
                kept_values[head, tile, slot, HEAD_SIZE:] = jnp.full(
                    value.shape, count.astype(jnp.bfloat16)
                )
        for tile in range(2):
            for member in range(GROUP):
                rows = pl.ds(tile * TILE, TILE)
                columns = pl.ds((head * GROUP + member) * HEAD_SIZE, HEAD_SIZE)
                scores = lax.dot_general(
                    q[rows, columns],
                    kept_keys[head, tile],
                    (((1,), (1,)), ((), ())),
                    preferred_element_type=jnp.float32,
                )
                scores = jnp.concatenate(
                    [scores[:, :TILE] + bias[tile], scores[:, TILE:]], axis=1
                )
                top = jnp.max(scores, axis=1, keepdims=True)
                weights = jnp.exp2((scores - top) * SCALE).astype(jnp.bfloat16)
                summed = jnp.dot(weights, kept_values[head, tile], preferred_element_type=jnp.float32)
                result = summed[:, :HEAD_SIZE] / summed[:, HEAD_SIZE:]
                out[rows, columns] = result.astype(jnp.bfloat16)


def pack_kernel(keys, values, own, tail, *parts):
    for head in range(KEY_VALUE_HEADS):
        columns = pl.ds(head * HEAD_SIZE, HEAD_SIZE)
        own[:, pl.ds(head * 2 * HEAD_SIZE, HEAD_SIZE)] = keys[:, columns]
        own[:, pl.ds((head * 2 + 1) * HEAD_SIZE, HEAD_SIZE)] = values[:, columns]
        tail[:, pl.ds(head * 2 * HEAD_SIZE, HEAD_SIZE)] = keys[TILE:, columns]
        tail[:, pl.ds((head * 2 + 1) * HEAD_SIZE, HEAD_SIZE)] = values[TILE:, columns]
    for (first, count), part in zip(HEAD_GROUPS, parts):
        for head in range(count):
            columns = pl.ds((first + head) * HEAD_SIZE, HEAD_SIZE)
            part[:, pl.ds(head * 2 * HEAD_SIZE, HEAD_SIZE)] = keys[:, columns]
            part[:, pl.ds((head * 2 + 1) * HEAD_SIZE, HEAD_SIZE)] = values[:, columns]


def pack(keys, values):
    whole = pl.BlockSpec(memory_space=pltpu.VMEM)
    widths = [count * 2 * HEAD_SIZE for _, count in HEAD_GROUPS]
    shapes = [(TOKENS, 2 * KEY_VALUE_HEADS * HEAD_SIZE), (TILE, 2 * KEY_VALUE_HEADS * HEAD_SIZE)]
    shapes += [(TOKENS, width) for width in widths]
    return pl.pallas_call(
        pack_kernel,
        out_shape=[jax.ShapeDtypeStruct(shape, jnp.bfloat16) for shape in shapes],
        in_specs=[whole, whole],
        out_specs=[whole] * len(shapes),
        name="pack",
    )(keys, values)


def attend(group, where, bias, queries, shared, own_group, previous):
    first_head, heads = group
    width = heads * GROUP * HEAD_SIZE
    part = heads * 2 * HEAD_SIZE
    number = first_head // heads
    whole = pl.BlockSpec(memory_space=pltpu.VMEM)
    tail, *shared = shared
    cross_tail, *own_group = own_group
    operands = [where, bias, queries, tail, cross_tail, *shared, *own_group]
    specs = [
        pl.BlockSpec(memory_space=pltpu.SMEM),
        whole,
        pl.BlockSpec((TOKENS, width), lambda i: (0, number)),
        pl.BlockSpec((TILE, part), lambda i: (0, number)),
        whole,
    ]
    specs += [pl.BlockSpec((TOKENS, part), lambda i: (0, number))] * len(shared)
    specs += [whole] * len(own_group)
    aliases = {}
    if previous is not None:
        aliases = {len(operands): 0}
        operands.append(previous)
        specs.append(pl.BlockSpec(memory_space=pl.ANY))
    scores = heads * GROUP * 2 * TILE * KEPT * TILE
    return pl.pallas_call(
        lambda *refs: attend_kernel(heads, first_head, *refs),
        grid=(1,),
        out_shape=jax.ShapeDtypeStruct(queries.shape, jnp.bfloat16),
        in_specs=specs,
        out_specs=pl.BlockSpec((TOKENS, width), lambda i: (0, number)),
        scratch_shapes=[
            pltpu.VMEM((heads, BLOCKS * TOKENS, HEAD_SIZE), jnp.bfloat16),
            pltpu.VMEM((heads, BLOCKS * TOKENS, HEAD_SIZE), jnp.bfloat16),
            pltpu.VMEM((heads, 2, KEPT * TILE, HEAD_SIZE), jnp.bfloat16),
            pltpu.VMEM((heads, 2, KEPT * TILE, 2 * HEAD_SIZE), jnp.bfloat16),
        ],
        input_output_aliases=aliases,
        compiler_params=pltpu.CompilerParams(vmem_limit_bytes=32 * 2**20),
        cost_estimate=pl.CostEstimate(
            flops=4 * scores * HEAD_SIZE, bytes_accessed=2 * 2**20, transcendentals=scores
        ),
        name="attend",
    )(*operands)


def shards(queries, keys, values, kept, frame_ids):
    chips = lax.axis_size("blk") // 2
    blk = lax.axis_index("blk")
    half = lax.axis_index("head")
    core = blk % 2

    def move(value, pairs):
        return lax.ppermute(value, AXES, pairs)

    own, last, *parts = pack(keys, values)
    crosses = [move(parts[0], across_halves(chips))]
    before = move(own, next_chip(chips))
    core_own = move(own, other_core(chips))
    tail = move(last, second_next_chip(chips, (0, 1)))
    tokens = lax.dynamic_slice_in_dim(frame_ids, (blk * 2 + half) * TOKENS, TOKENS, 0)
    frames = tokens.reshape(2, TILE)
    bias = jnp.where(frames[:, None, :] <= frames[:, :, None], 0.0, NEVER).astype(jnp.float32)
    rows = lax.dynamic_slice_in_dim(kept, half * 2, 2, 0) - (blk // 2) * 8 + 12
    other = 1 - core
    far = 1 - half
    near = jnp.where(turns(blk // 2), far, half)
    slots = jnp.stack(
        [
            6 + 2 * core + half,
            2 + 2 * core + near,
            6 + 2 * other + half,
            2 + 2 * other + near,
            6 + 2 * core + far,
            2 + 2 * core + 1 - near,
            6 + 2 * other + far,
            2 + 2 * other + 1 - near,
            (2 * half + 1) * TILE,
        ]
    )
    where = jnp.zeros((3, 16), jnp.int32)
    where = lax.dynamic_update_slice(where, rows, (0, 0))
    where = lax.dynamic_update_slice(where, slots[None, :].astype(jnp.int32), (2, 0))

    before, core_own, tail = lax.optimization_barrier((before, core_own, tail))
    core_before = move(before, other_core(chips))
    result = None
    waited = (before, core_own, tail)
    for number, group in enumerate(HEAD_GROUPS):
        cross = crosses[number]
        if number + 1 < len(HEAD_GROUPS):
            sent, waited = lax.optimization_barrier((parts[number + 1], waited))
            crosses.append(move(sent, across_halves(chips)))
        cross_before = move(cross, next_chip(chips))
        core_cross = move(cross, other_core(chips))
        cross_tail = move(cross, second_next_chip(chips, (0,)))
        if number + 1 < len(HEAD_GROUPS):
            (cross_before, core_cross, cross_tail, core_before, crosses[-1]) = (
                lax.optimization_barrier(
                    (cross_before, core_cross, cross_tail, core_before, crosses[-1])
                )
            )
        core_cross_before = move(cross_before, other_core(chips))
        shared = (tail, own, before, core_own, core_before)
        own_group = (cross_tail, cross, cross_before, core_cross, core_cross_before)
        result = attend(group, where, bias, queries, shared, own_group, result)
    return result


def solution(mesh):
    placed = (
        P(AXES, None),
        P(AXES, None),
        P(AXES, None),
        P("blk", None),
        P(),
    )
    return jax.shard_map(
        shards, mesh=mesh, in_specs=placed, out_specs=P(AXES, None), check_vma=False
    )
```

```python
import math

import jax
import jax.numpy as jnp
from jax import lax
from jax.experimental import pallas as pl
from jax.experimental.pallas import tpu as pltpu
from jax.sharding import PartitionSpec as P

QUERY_HEADS = 28
KEY_VALUE_HEADS = 4
GROUP = QUERY_HEADS // KEY_VALUE_HEADS
HEAD_SIZE = 128
PAIR = 2 * HEAD_SIZE
TILE = 128
TOKENS = 256
KEPT = 8
REACH = 6
AXES = ("blk", "head")
HEAD_GROUPS = ((0, 2), (2, 2))
SCALE = math.log2(math.e) / math.sqrt(HEAD_SIZE)
NEVER = -1e30


def pack_kernel(keys, values, own, *parts):
    for (first, count), target in zip(((0, KEY_VALUE_HEADS),), (own, *parts)):
        for head in range(count):
            columns = pl.ds((first + head) * HEAD_SIZE, HEAD_SIZE)
            target[:, pl.ds(head * PAIR, HEAD_SIZE)] = keys[:, columns]
            target[:, pl.ds(head * PAIR + HEAD_SIZE, HEAD_SIZE)] = values[:, columns]


def pack(keys, values):
    whole = pl.BlockSpec(memory_space=pltpu.VMEM)
    widths = [KEY_VALUE_HEADS * PAIR]
    return pl.pallas_call(
        pack_kernel,
        out_shape=[pltpu.VMEM((TOKENS, width), jnp.bfloat16) for width in widths],
        in_specs=[whole, whole],
        out_specs=[whole] * len(widths),
        name="pack",
    )(keys, values)


def attend_kernel(first_head, heads, kept, bias, queries, *refs):
    blocks = refs[: REACH + 1]
    out, q, rows_kept, keys, values, kept_keys, kept_values, arrived = refs[-8:]
    blk = lax.axis_index("blk")
    half = lax.axis_index("head")
    width = heads * GROUP * HEAD_SIZE
    first = first_head * GROUP * HEAD_SIZE
    listed = pltpu.make_async_copy(kept, rows_kept, arrived.at[0])
    listed.start()
    fetch = pltpu.make_async_copy(queries.at[:, pl.ds(first, width)], q, arrived.at[1])
    fetch.start()
    origin = (blk * 2 + half - REACH) * (TOKENS // TILE)

    def gather(head):
        for behind, block in enumerate(blocks):
            skip = TOKENS - block.shape[0]
            rows = pl.ds((REACH - behind) * TOKENS + skip, block.shape[0])
            keys[head, rows, :] = block[:, pl.ds(head * PAIR, HEAD_SIZE)]
            values[head, rows, :] = block[:, pl.ds(head * PAIR + HEAD_SIZE, HEAD_SIZE)]
        if head == 0:
            listed.wait()
        for tile in range(2):
            entries = [rows_kept[half * 2 + tile, entry] - origin for entry in range(KEPT)]
            for entry, index in enumerate(entries):
                rows = pl.ds(pl.multiple_of(index * TILE, TILE), TILE)
                slot = pl.ds(entry * TILE, TILE)
                key = keys[head, rows, :]
                value = values[head, rows, :]
                count = jnp.float32(1.0)
                if entry:
                    again = index == entries[0]
                    key = jnp.where(again, jnp.broadcast_to(key[0:1, :], key.shape), key)
                    for earlier in entries[1:entry]:
                        again = again | (index == earlier)
                    value = jnp.where(again, jnp.zeros_like(value), value)
                    count = jnp.where(again, 0.0, 1.0)
                kept_keys[head, tile, slot, :] = key
                kept_values[head, tile, slot, :HEAD_SIZE] = value
                kept_values[head, tile, slot, HEAD_SIZE:] = jnp.full(
                    value.shape, count.astype(jnp.bfloat16)
                )

    for head in range(heads):
        gather(head)
        if head == 0:
            fetch.wait()
        for tile in range(2):
            for member in range(GROUP):
                rows = pl.ds(tile * TILE, TILE)
                columns = pl.ds((head * GROUP + member) * HEAD_SIZE, HEAD_SIZE)
                scores = lax.dot_general(
                    q[rows, columns],
                    kept_keys[head, tile],
                    (((1,), (1,)), ((), ())),
                    preferred_element_type=jnp.float32,
                )
                scores = jnp.concatenate(
                    [scores[:, :TILE] + bias[tile], scores[:, TILE:]], axis=1
                )
                top = jnp.max(scores, axis=1, keepdims=True)
                weights = jnp.exp2((scores - top) * SCALE).astype(jnp.bfloat16)
                summed = jnp.dot(
                    weights, kept_values[head, tile], preferred_element_type=jnp.float32
                )
                result = summed[:, :HEAD_SIZE] / summed[:, HEAD_SIZE:]
                out[rows, columns] = result.astype(jnp.bfloat16)


def attend(group, kept, bias, queries, blocks, previous):
    first_head, heads = group
    width = heads * GROUP * HEAD_SIZE
    part = heads * PAIR
    number = first_head // heads
    whole = pl.BlockSpec(memory_space=pltpu.VMEM)
    queries = pltpu.with_memory_space_constraint(queries, pltpu.HBM)
    kept = pltpu.with_memory_space_constraint(kept, pltpu.HBM)
    operands = [kept, bias, queries, *blocks]
    specs = [
        pl.BlockSpec(memory_space=pltpu.HBM),
        whole,
        pl.BlockSpec(memory_space=pltpu.HBM),
    ]
    for block in blocks:
        if block.shape[1] == part:
            specs.append(whole)
        else:
            specs.append(pl.BlockSpec((block.shape[0], part), lambda i: (0, number)))
    aliases = {}
    if previous is not None:
        aliases = {len(operands): 0}
        operands.append(previous)
        specs.append(pl.BlockSpec(memory_space=pl.ANY))
    return pl.pallas_call(
        lambda *refs: attend_kernel(first_head, heads, *refs),
        grid=(1,),
        out_shape=jax.ShapeDtypeStruct(queries.shape, jnp.bfloat16),
        in_specs=specs,
        out_specs=pl.BlockSpec((TOKENS, width), lambda i: (0, number)),
        scratch_shapes=[
            pltpu.VMEM((TOKENS, width), jnp.bfloat16),
            pltpu.SMEM((2 * 2, KEPT), jnp.int32),
            pltpu.VMEM((heads, (REACH + 1) * TOKENS, HEAD_SIZE), jnp.bfloat16),
            pltpu.VMEM((heads, (REACH + 1) * TOKENS, HEAD_SIZE), jnp.bfloat16),
            pltpu.VMEM((heads, 2, KEPT * TILE, HEAD_SIZE), jnp.bfloat16),
            pltpu.VMEM((heads, 2, KEPT * TILE, 2 * HEAD_SIZE), jnp.bfloat16),
            pltpu.SemaphoreType.DMA((2,)),
        ],
        input_output_aliases=aliases,
        compiler_params=pltpu.CompilerParams(vmem_limit_bytes=32 * 2**20),
        cost_estimate=pl.CostEstimate(flops=2**20, bytes_accessed=2**16, transcendentals=0),
        name="attend",
    )(*operands)


def shards(queries, keys, values, kept, frame_ids):
    blk = lax.axis_index("blk")
    half = lax.axis_index("head")
    devices = lax.axis_size("blk") * 2

    def ahead(value, blocks):
        pairs = [(source, (source + blocks) % devices) for source in range(devices)]
        return lax.ppermute(value, AXES, pairs)

    tokens = lax.dynamic_slice_in_dim(frame_ids, (blk * 2 + half) * TOKENS, TOKENS, 0)
    frames = tokens.reshape(2, TILE)
    bias = jnp.where(frames[:, None, :] <= frames[:, :, None], 0.0, NEVER).astype(jnp.float32)

    (own,) = pack(keys, values)
    both_1 = ahead(own, 1)
    both_2 = ahead(own, 2)
    both_4 = ahead(both_2, 2)
    both_1, bias = lax.optimization_barrier((both_1, bias))
    width = HEAD_GROUPS[0][1] * PAIR
    first_3 = ahead(both_1[:, :width], 2)
    second_3 = ahead(both_1[:, width:], 2)
    both_6 = ahead(both_4[TILE:], 2)
    first_3, second_3 = lax.optimization_barrier((first_3, second_3))
    first_5 = ahead(first_3, 2)
    both_6, first_5 = lax.optimization_barrier((both_6, first_5))
    second_5 = ahead(second_3, 2)
    blocks = (own, both_1, both_2, first_3, both_4, first_5, both_6)
    result = attend(HEAD_GROUPS[0], kept, bias, queries, blocks, None)
    second_5, result = lax.optimization_barrier((second_5, result))
    blocks = (own, both_1, both_2, second_3, both_4, second_5, both_6)
    return attend(HEAD_GROUPS[1], kept, bias, queries, blocks, result)


def solution(mesh):
    placed = (
        P(AXES, None),
        P(AXES, None),
        P(AXES, None),
        P("blk", None),
        P(),
    )
    return jax.shard_map(
        shards, mesh=mesh, in_specs=placed, out_specs=P(AXES, None), check_vma=False
    )
```

```python
import math

import jax
import jax.numpy as jnp
from jax import lax
from jax.experimental import pallas as pl
from jax.experimental.pallas import tpu as pltpu
from jax.sharding import PartitionSpec as P

QUERY_HEADS = 28
KEY_VALUE_HEADS = 4
GROUP = QUERY_HEADS // KEY_VALUE_HEADS
HEAD_SIZE = 128
PAIR = 2 * HEAD_SIZE
TILE = 128
TOKENS = 256
KEPT = 8
REACH = 6
AXES = ("blk", "head")
HEAD_GROUPS = ((0, 2), (2, 2))
SCALE = math.log2(math.e) / math.sqrt(HEAD_SIZE)
NEVER = -1e30


def pack_kernel(keys, values, own, *parts):
    for (first, count), target in zip(((0, KEY_VALUE_HEADS),), (own, *parts)):
        for head in range(count):
            columns = pl.ds((first + head) * HEAD_SIZE, HEAD_SIZE)
            target[:, pl.ds(head * PAIR, HEAD_SIZE)] = keys[:, columns]
            target[:, pl.ds(head * PAIR + HEAD_SIZE, HEAD_SIZE)] = values[:, columns]


def pack(keys, values):
    whole = pl.BlockSpec(memory_space=pltpu.VMEM)
    widths = [KEY_VALUE_HEADS * PAIR]
    return pl.pallas_call(
        pack_kernel,
        out_shape=[pltpu.VMEM((TOKENS, width), jnp.bfloat16) for width in widths],
        in_specs=[whole, whole],
        out_specs=[whole] * len(widths),
        name="pack",
    )(keys, values)


def attend_kernel(first_head, heads, kept, bias, queries, *refs):
    blocks = refs[: REACH + 1]
    out, q, rows_kept, keys, values, kept_keys, kept_values, arrived = refs[-8:]
    blk = lax.axis_index("blk")
    half = lax.axis_index("head")
    width = heads * GROUP * HEAD_SIZE
    first = first_head * GROUP * HEAD_SIZE
    listed = pltpu.make_async_copy(kept, rows_kept, arrived.at[0])
    listed.start()
    fetch = pltpu.make_async_copy(queries.at[:, pl.ds(first, width)], q, arrived.at[1])
    fetch.start()
    origin = (blk * 2 + half - REACH) * (TOKENS // TILE)

    def gather(head):
        for behind, block in enumerate(blocks):
            skip = TOKENS - block.shape[0]
            rows = pl.ds((REACH - behind) * TOKENS + skip, block.shape[0])
            keys[head, rows, :] = block[:, pl.ds(head * PAIR, HEAD_SIZE)]
            values[head, rows, :] = block[:, pl.ds(head * PAIR + HEAD_SIZE, HEAD_SIZE)]
        if head == 0:
            listed.wait()
        for tile in range(2):
            entries = [rows_kept[half * 2 + tile, entry] - origin for entry in range(KEPT)]
            for entry, index in enumerate(entries):
                rows = pl.ds(pl.multiple_of(index * TILE, TILE), TILE)
                slot = pl.ds(entry * TILE, TILE)
                key = keys[head, rows, :]
                value = values[head, rows, :]
                count = jnp.float32(1.0)
                if entry:
                    again = index == entries[0]
                    key = jnp.where(again, jnp.broadcast_to(key[0:1, :], key.shape), key)
                    for earlier in entries[1:entry]:
                        again = again | (index == earlier)
                    value = jnp.where(again, jnp.zeros_like(value), value)
                    count = jnp.where(again, 0.0, 1.0)
                kept_keys[head, tile, slot, :] = key
                kept_values[head, tile, slot, :HEAD_SIZE] = value
                kept_values[head, tile, slot, HEAD_SIZE:] = jnp.full(
                    value.shape, count.astype(jnp.bfloat16)
                )

    for head in range(heads):
        gather(head)
        if head == 0:
            fetch.wait()
        for tile in range(2):
            for member in range(GROUP):
                rows = pl.ds(tile * TILE, TILE)
                columns = pl.ds((head * GROUP + member) * HEAD_SIZE, HEAD_SIZE)
                scores = lax.dot_general(
                    q[rows, columns],
                    kept_keys[head, tile],
                    (((1,), (1,)), ((), ())),
                    preferred_element_type=jnp.float32,
                )
                scores = jnp.concatenate(
                    [scores[:, :TILE] + bias[tile], scores[:, TILE:]], axis=1
                )
                top = jnp.max(scores, axis=1, keepdims=True)
                weights = jnp.exp2((scores - top) * SCALE).astype(jnp.bfloat16)
                summed = jnp.dot(
                    weights, kept_values[head, tile], preferred_element_type=jnp.float32
                )
                result = summed[:, :HEAD_SIZE] / summed[:, HEAD_SIZE:]
                out[rows, columns] = result.astype(jnp.bfloat16)


def attend(group, kept, bias, queries, blocks, previous):
    first_head, heads = group
    width = heads * GROUP * HEAD_SIZE
    part = heads * PAIR
    number = first_head // heads
    whole = pl.BlockSpec(memory_space=pltpu.VMEM)
    queries = pltpu.with_memory_space_constraint(queries, pltpu.HBM)
    kept = pltpu.with_memory_space_constraint(kept, pltpu.HBM)
    operands = [kept, bias, queries, *blocks]
    specs = [
        pl.BlockSpec(memory_space=pltpu.HBM),
        whole,
        pl.BlockSpec(memory_space=pltpu.HBM),
    ]
    for block in blocks:
        if block.shape[1] == part:
            specs.append(whole)
        else:
            specs.append(pl.BlockSpec((block.shape[0], part), lambda i: (0, number)))
    aliases = {}
    if previous is not None:
        aliases = {len(operands): 0}
        operands.append(previous)
        specs.append(pl.BlockSpec(memory_space=pl.ANY))
    return pl.pallas_call(
        lambda *refs: attend_kernel(first_head, heads, *refs),
        grid=(1,),
        out_shape=jax.ShapeDtypeStruct(queries.shape, jnp.bfloat16),
        in_specs=specs,
        out_specs=pl.BlockSpec((TOKENS, width), lambda i: (0, number)),
        scratch_shapes=[
            pltpu.VMEM((TOKENS, width), jnp.bfloat16),
            pltpu.SMEM((2 * 2, KEPT), jnp.int32),
            pltpu.VMEM((heads, (REACH + 1) * TOKENS, HEAD_SIZE), jnp.bfloat16),
            pltpu.VMEM((heads, (REACH + 1) * TOKENS, HEAD_SIZE), jnp.bfloat16),
            pltpu.VMEM((heads, 2, KEPT * TILE, HEAD_SIZE), jnp.bfloat16),
            pltpu.VMEM((heads, 2, KEPT * TILE, 2 * HEAD_SIZE), jnp.bfloat16),
            pltpu.SemaphoreType.DMA((2,)),
        ],
        input_output_aliases=aliases,
        compiler_params=pltpu.CompilerParams(vmem_limit_bytes=32 * 2**20),
        cost_estimate=pl.CostEstimate(flops=2**20, bytes_accessed=2**16, transcendentals=0),
        name="attend",
    )(*operands)


def shards(queries, keys, values, kept, frame_ids):
    blk = lax.axis_index("blk")
    half = lax.axis_index("head")
    devices = lax.axis_size("blk") * 2

    def ahead(value, blocks, spare=()):
        first = blocks + len(spare)
        pairs = [(target - blocks, target) for target in range(first, devices)]
        around = [target for target in range(first) if target not in spare]
        pairs += [(devices - blocks + i, target) for i, target in enumerate(around)]
        pairs += list(enumerate(spare))
        return lax.ppermute(value, AXES, pairs)

    tokens = lax.dynamic_slice_in_dim(frame_ids, (blk * 2 + half) * TOKENS, TOKENS, 0)
    frames = tokens.reshape(2, TILE)
    bias = jnp.where(frames[:, None, :] <= frames[:, :, None], 0.0, NEVER).astype(jnp.float32)

    (own,) = pack(keys, values)
    both_1 = ahead(own, 1)
    both_2 = ahead(own, 2)
    both_4 = ahead(both_2, 2, (1, 0))
    both_1, bias = lax.optimization_barrier((both_1, bias))
    width = HEAD_GROUPS[0][1] * PAIR
    first_3 = ahead(both_1[:, :width], 2, (2,))
    second_3 = ahead(both_1[:, width:], 2, (2,))
    both_6 = ahead(both_4[TILE:], 2, (2, 3, 0, 1))
    first_3, second_3 = lax.optimization_barrier((first_3, second_3))
    first_5 = ahead(first_3, 2, (2, 3, 0))
    both_6, first_5 = lax.optimization_barrier((both_6, first_5))
    second_5 = ahead(second_3, 2, (2, 3, 0))
    blocks = (own, both_1, both_2, first_3, both_4, first_5, both_6)
    result = attend(HEAD_GROUPS[0], kept, bias, queries, blocks, None)
    second_5, result = lax.optimization_barrier((second_5, result))
    blocks = (own, both_1, both_2, second_3, both_4, second_5, both_6)
    return attend(HEAD_GROUPS[1], kept, bias, queries, blocks, result)


def solution(mesh):
    placed = (
        P(AXES, None),
        P(AXES, None),
        P(AXES, None),
        P("blk", None),
        P(),
    )
    return jax.shard_map(
        shards, mesh=mesh, in_specs=placed, out_specs=P(AXES, None), check_vma=False
    )
```

```python
import math

import jax
import jax.numpy as jnp
from jax import lax
from jax.experimental import pallas as pl
from jax.experimental.pallas import tpu as pltpu
from jax.sharding import PartitionSpec as P

QUERY_HEADS = 28
KEY_VALUE_HEADS = 4
GROUP = QUERY_HEADS // KEY_VALUE_HEADS
HEAD_SIZE = 128
PAIR = 2 * HEAD_SIZE
TILE = 128
TOKENS = 256
KEPT = 8
REACH = 6
AXES = ("blk", "head")
HEAD_GROUPS = ((0, 2), (2, 2))
SCALE = math.log2(math.e) / math.sqrt(HEAD_SIZE)
NEVER = -1e30


def pack_kernel(keys, values, own, *parts):
    for (first, count), target in zip(((0, KEY_VALUE_HEADS),), (own, *parts)):
        for head in range(count):
            columns = pl.ds((first + head) * HEAD_SIZE, HEAD_SIZE)
            target[:, pl.ds(head * PAIR, HEAD_SIZE)] = keys[:, columns]
            target[:, pl.ds(head * PAIR + HEAD_SIZE, HEAD_SIZE)] = values[:, columns]


def pack(keys, values):
    whole = pl.BlockSpec(memory_space=pltpu.VMEM)
    widths = [KEY_VALUE_HEADS * PAIR]
    return pl.pallas_call(
        pack_kernel,
        out_shape=[pltpu.VMEM((TOKENS, width), jnp.bfloat16) for width in widths],
        in_specs=[whole, whole],
        out_specs=[whole] * len(widths),
        name="pack",
    )(keys, values)


def attend_kernel(first_head, heads, kept, bias, queries, *refs):
    blocks = refs[: REACH + 1]
    out, q, rows_kept, keys, values, kept_keys, kept_values, arrived = refs[-8:]
    blk = lax.axis_index("blk")
    half = lax.axis_index("head")
    width = heads * GROUP * HEAD_SIZE
    first = first_head * GROUP * HEAD_SIZE
    listed = pltpu.make_async_copy(kept, rows_kept, arrived.at[0])
    listed.start()
    fetch = pltpu.make_async_copy(queries.at[:, pl.ds(first, width)], q, arrived.at[1])
    fetch.start()
    origin = (blk * 2 + half - REACH) * (TOKENS // TILE)

    def gather(head):
        for behind, block in enumerate(blocks):
            skip = TOKENS - block.shape[0]
            rows = pl.ds((REACH - behind) * TOKENS + skip, block.shape[0])
            keys[head, rows, :] = block[:, pl.ds(head * PAIR, HEAD_SIZE)]
            values[head, rows, :] = block[:, pl.ds(head * PAIR + HEAD_SIZE, HEAD_SIZE)]
        if head == 0:
            listed.wait()
        for tile in range(2):
            entries = [rows_kept[half * 2 + tile, entry] - origin for entry in range(KEPT)]
            for entry, index in enumerate(entries):
                rows = pl.ds(pl.multiple_of(index * TILE, TILE), TILE)
                slot = pl.ds(entry * TILE, TILE)
                key = keys[head, rows, :]
                value = values[head, rows, :]
                count = jnp.float32(1.0)
                if entry:
                    again = index == entries[0]
                    key = jnp.where(again, jnp.broadcast_to(key[0:1, :], key.shape), key)
                    for earlier in entries[1:entry]:
                        again = again | (index == earlier)
                    value = jnp.where(again, jnp.zeros_like(value), value)
                    count = jnp.where(again, 0.0, 1.0)
                kept_keys[head, tile, slot, :] = key
                kept_values[head, tile, slot, :HEAD_SIZE] = value
                kept_values[head, tile, slot, HEAD_SIZE:] = jnp.full(
                    value.shape, count.astype(jnp.bfloat16)
                )

    for head in range(heads):
        gather(head)
        if head == 0:
            fetch.wait()
        for member in range(GROUP):
            for tile in range(2):
                rows = pl.ds(tile * TILE, TILE)
                columns = pl.ds((head * GROUP + member) * HEAD_SIZE, HEAD_SIZE)
                scores = lax.dot_general(
                    q[rows, columns],
                    kept_keys[head, tile],
                    (((1,), (1,)), ((), ())),
                    preferred_element_type=jnp.float32,
                )
                scores = jnp.concatenate(
                    [scores[:, :TILE] + bias[tile], scores[:, TILE:]], axis=1
                )
                top = jnp.max(scores, axis=1, keepdims=True)
                weights = jnp.exp2((scores - top) * SCALE).astype(jnp.bfloat16)
                summed = jnp.dot(
                    weights, kept_values[head, tile], preferred_element_type=jnp.float32
                )
                result = summed[:, :HEAD_SIZE] / summed[:, HEAD_SIZE:]
                out[rows, columns] = result.astype(jnp.bfloat16)


def attend(group, kept, bias, queries, blocks, previous):
    first_head, heads = group
    width = heads * GROUP * HEAD_SIZE
    part = heads * PAIR
    number = first_head // heads
    whole = pl.BlockSpec(memory_space=pltpu.VMEM)
    queries = pltpu.with_memory_space_constraint(queries, pltpu.HBM)
    kept = pltpu.with_memory_space_constraint(kept, pltpu.HBM)
    operands = [kept, bias, queries, *blocks]
    specs = [
        pl.BlockSpec(memory_space=pltpu.HBM),
        whole,
        pl.BlockSpec(memory_space=pltpu.HBM),
    ]
    for block in blocks:
        if block.shape[1] == part:
            specs.append(whole)
        else:
            specs.append(pl.BlockSpec((block.shape[0], part), lambda i: (0, number)))
    aliases = {}
    if previous is not None:
        aliases = {len(operands): 0}
        operands.append(previous)
        specs.append(pl.BlockSpec(memory_space=pl.ANY))
    return pl.pallas_call(
        lambda *refs: attend_kernel(first_head, heads, *refs),
        grid=(1,),
        out_shape=jax.ShapeDtypeStruct(queries.shape, jnp.bfloat16),
        in_specs=specs,
        out_specs=pl.BlockSpec((TOKENS, width), lambda i: (0, number)),
        scratch_shapes=[
            pltpu.VMEM((TOKENS, width), jnp.bfloat16),
            pltpu.SMEM((2 * 2, KEPT), jnp.int32),
            pltpu.VMEM((heads, (REACH + 1) * TOKENS, HEAD_SIZE), jnp.bfloat16),
            pltpu.VMEM((heads, (REACH + 1) * TOKENS, HEAD_SIZE), jnp.bfloat16),
            pltpu.VMEM((heads, 2, KEPT * TILE, HEAD_SIZE), jnp.bfloat16),
            pltpu.VMEM((heads, 2, KEPT * TILE, 2 * HEAD_SIZE), jnp.bfloat16),
            pltpu.SemaphoreType.DMA((2,)),
        ],
        input_output_aliases=aliases,
        compiler_params=pltpu.CompilerParams(vmem_limit_bytes=32 * 2**20),
        cost_estimate=pl.CostEstimate(flops=2**20, bytes_accessed=2**16, transcendentals=0),
        name="attend",
    )(*operands)


def shards(queries, keys, values, kept, frame_ids):
    blk = lax.axis_index("blk")
    half = lax.axis_index("head")
    devices = lax.axis_size("blk") * 2

    def ahead(value, blocks, spare=()):
        first = blocks + len(spare)
        pairs = [(target - blocks, target) for target in range(first, devices)]
        around = [target for target in range(first) if target not in spare]
        pairs += [(devices - blocks + i, target) for i, target in enumerate(around)]
        pairs += list(enumerate(spare))
        return lax.ppermute(value, AXES, pairs)

    tokens = lax.dynamic_slice_in_dim(frame_ids, (blk * 2 + half) * TOKENS, TOKENS, 0)
    frames = tokens.reshape(2, TILE)
    bias = jnp.where(frames[:, None, :] <= frames[:, :, None], 0.0, NEVER).astype(jnp.float32)

    (own,) = pack(keys, values)
    both_1 = ahead(own, 1)
    both_2 = ahead(own, 2)
    both_4 = ahead(both_2, 2, (1, 0))
    both_1, bias = lax.optimization_barrier((both_1, bias))
    width = HEAD_GROUPS[0][1] * PAIR
    first_3 = ahead(both_1[:, :width], 2, (2,))
    second_3 = ahead(both_1[:, width:], 2, (2,))
    both_6 = ahead(both_4[TILE:], 2, (2, 3, 0, 1))
    first_3, second_3 = lax.optimization_barrier((first_3, second_3))
    first_5 = ahead(first_3, 2, (2, 3, 0))
    both_6, first_5 = lax.optimization_barrier((both_6, first_5))
    second_5 = ahead(second_3, 2, (2, 3, 0))
    blocks = (own, both_1, both_2, first_3, both_4, first_5, both_6)
    result = attend(HEAD_GROUPS[0], kept, bias, queries, blocks, None)
    second_5, result = lax.optimization_barrier((second_5, result))
    blocks = (own, both_1, both_2, second_3, both_4, second_5, both_6)
    return attend(HEAD_GROUPS[1], kept, bias, queries, blocks, result)


def solution(mesh):
    placed = (
        P(AXES, None),
        P(AXES, None),
        P(AXES, None),
        P("blk", None),
        P(),
    )
    return jax.shard_map(
        shards, mesh=mesh, in_specs=placed, out_specs=P(AXES, None), check_vma=False
    )
```
